256 devices in a mesh: row: 8 (over z), slab: 16 (over x, y), rep: 2 (over core).
Axes of the slice: x: 4, y: 4, z: 8, core: 2. Of those that a mesh axis runs over, the one named last changes fastest.
Arguments:
- t2_stored: float32 [4096, 40960], P('row', ('slab', 'rep')), may hold values from -6 to 6
- v_slab: float32 [1536, 40960], P('rep', 'slab'), may hold values from -0.03125 to 0.03125
- block_source: int32 [320], replicated, may hold values from 0 to 319, as said below
- r_in: float32 [4096, 1536], P(('row', 'slab'), 'rep'), may hold values from -6 to 6
Outputs:
- r_out: float32 [4096, 1536], P(('row', 'slab'), 'rep')
The draws below stay inside these ranges and needn't reach their ends.
Inputs may be any that keep to these rules, and one draw needn't show every extreme that they name: block_source is a permutation of the 320 stored blocks. Slab index t owns the blocks k with k // 20 == t; stored block q lies on the device of slab and rep numbered q // 10. Every such device stores either none or exactly 2 blocks owned by any one slab index, and the slab indices it stores blocks for form a run of 5 consecutive indices counted modulo the slab axis.
All inputs are finite; a program needn't handle non-finite values.
Results may differ from the reference program's by a relative error of at most 0.000084.
Values sent between devices are 32-bit elements; how exact they have to be, the bound alone decides.
A program may use at most 128 MiB of HBM per device.

```python
import jax
import jax.numpy as jnp
from jax import lax

IJ_DEV = 512
AB = 1536
CD = 40960
BLK = 128
NIJ = 4096
NBLK = 320
STORED = 10
CAP = 2
N_ROW = 8
N_SLAB = 16
N_REP = 2


def draw_block_source(key, part):
    key = jax.random.fold_in(key, 7)
    key_start, key_local, key_order = jax.random.split(key, 3)
    holders = N_SLAB * N_REP
    starts = jax.random.permutation(key_start, holders).astype(jnp.int32) % N_SLAB
    places = jnp.arange(STORED, dtype=jnp.int32)
    scores = jax.random.randint(key_local, (holders, STORED), 0, 1 << 20) * STORED + places[None, :]
    shuffle = jnp.argsort(scores, axis=1, stable=True).astype(jnp.int32)
    owners = (starts[:, None] + shuffle // CAP) % N_SLAB
    owners = owners.reshape(NBLK)
    mixing = jax.random.permutation(key_order, NBLK).astype(jnp.int32)
    order_key = owners * NBLK + mixing
    return jnp.argsort(order_key, stable=True).astype(jnp.int32)


def level_of(key, extent, shards, low, high):
    def one(dim, parts):
        draws = jax.random.uniform(jax.random.fold_in(jax.random.fold_in(key, 6), dim), (parts,), jnp.float32, low / len(shards), high / len(shards))
        return jnp.repeat(jnp.exp(draws), extent[dim] // parts).reshape((-1,) + (1,) * (len(extent) - dim - 1))

    factor_of = one(*shards[0])
    for cut in shards[1:]:
        factor_of = factor_of * one(*cut)
    return factor_of


def gaussian(own_key, dims, width, bound, cuts=(), held_as=jnp.bfloat16):
    entries = width * jax.random.normal(own_key, dims, jnp.float32)
    if cuts:
        entries = entries * level_of(own_key, dims, cuts, -0.22, 0.18)
    return jnp.clip(entries, -bound, bound).astype(held_as)


def setup_inputs(seed: int = 0) -> dict:
    key_of = jax.random.split(jax.random.key(seed), 5)
    return {
        "t2_stored": gaussian(key_of[0], (NIJ, CD), 1.0, 6.0, ((0, 8), (1, 32)), jnp.float32),
        "v_slab": gaussian(key_of[1], (AB, CD), CD ** -0.5, 0.03125, ((0, 2), (1, 16)), jnp.float32),
        "block_source": draw_block_source(jax.random.fold_in(key_of[4], 71), 0),
        "r_in": gaussian(key_of[3], (NIJ, AB), 1.0, 6.0, ((0, 128), (1, 2)), jnp.float32),
    }


def reference(t2_stored, v_slab, block_source, r_in):
    def ladder_rows(slab_rows):
        blocked = slab_rows.reshape(IJ_DEV, NBLK, BLK)
        ordered = jnp.take(blocked, block_source.astype(jnp.int32), axis=1).reshape(IJ_DEV, CD)
        return lax.dot_general(ordered, v_slab, (((1,), (1,)), ((), ())),
                               precision=lax.Precision.HIGHEST,
                               preferred_element_type=jnp.float32)

    ladder = lax.map(ladder_rows, t2_stored.reshape(N_ROW, IJ_DEV, CD)).reshape(NIJ, AB)
    return r_in + ladder
```

```python
import jax
import jax.numpy as jnp
from jax import lax
from jax.experimental import pallas as pl
from jax.experimental.pallas import tpu as pltpu
from jax.sharding import PartitionSpec as P

BLK = 128
SIDE = 4
SLABS = 16
CHUNKS = 2
ROWS = 8
MESH = pl.DeviceIdType.MESH


def hops(da, db):
    return min(da, SIDE - da) + min(db, SIDE - db)


SHIFTS = sorted(
    [(da, db) for da in range(SIDE) for db in range(SIDE)],
    key=lambda d: -hops(*d),
)


def slot(da, db):
    return da * SIDE + db


def kernel(
    source_ref, t2_ref, v_ref, r_ref, out_ref,
    v_raw, v_hi, v_lo, part_a, part_b, send_buf, whole, split, ladder, level1, summed, level2,
    v_sem, own_sem, send1, recv1, send2, recv2, send3, recv3, send4, recv4, send5, recv5,
):
    row = lax.axis_index("row")
    slab = lax.axis_index("slab")
    core = lax.axis_index("rep")
    x, y = slab // SIDE, slab % SIDE
    a = x + core * (y - x)
    b = y + core * (x - y)
    stored = t2_ref.shape[1]
    owned = v_ref.shape[1] // BLK
    strip = CHUNKS * ROWS
    parts = (part_a, part_b)

    def slab_at(da, db):
        aa, bb = (a + da + SIDE) % SIDE, (b + db + SIDE) % SIDE
        xx, yy = aa + core * (bb - aa), bb + core * (aa - bb)
        return xx * SIDE + yy

    def device(da, db, flip=0):
        return (row, slab_at(da, db), (core + flip) % 2)

    v_copy = pltpu.make_async_copy(v_ref, v_raw, v_sem)
    v_copy.start()

    def spread(chunk, da, db, flip):
        to_slab = slab_at(da, db)
        to_core = (core + flip) % 2
        rows = t2_ref.at[(to_slab * 2 + to_core) * CHUNKS + chunk]
        here = pl.ds((slab * 2 + core) * stored, stored)
        n = slot(da, db) * 2 + flip
        if da == 0 and db == 0 and flip == 0:
            return pltpu.make_async_copy(rows, parts[chunk].at[here], own_sem.at[chunk])
        return pltpu.make_async_remote_copy(
            src_ref=rows,
            dst_ref=parts[chunk].at[here],
            send_sem=send1.at[chunk, n],
            recv_sem=recv1.at[chunk, n],
            device_id=device(da, db, flip),
            device_id_type=MESH,
        )

    def spread_arrival(chunk, da, db, flip):
        from_slab = slab_at(-da, -db)
        n = slot(da, db) * 2 + flip
        if flip:
            from_slab = slab_at(-db, -da)
        there = pl.ds((from_slab * 2 + (core + flip) % 2) * stored, stored)
        return pltpu.make_async_remote_copy(
            src_ref=parts[chunk].at[there],
            dst_ref=parts[chunk].at[there],
            send_sem=send1.at[chunk, n],
            recv_sem=recv1.at[chunk, n],
            device_id=device(da, db, flip),
            device_id_type=MESH,
        )

    def collect(chunk, da, db):
        n = slot(da, db)
        return pltpu.make_async_remote_copy(
            src_ref=send_buf.at[chunk, n],
            dst_ref=whole.at[chunk, pl.ds(n * strip, ROWS)],
            send_sem=send2.at[chunk, n],
            recv_sem=recv2.at[chunk, n],
            device_id=device(da, db),
            device_id_type=MESH,
        )

    def share(chunk, da, db):
        return pltpu.make_async_remote_copy(
            src_ref=whole.at[chunk, pl.ds(slot(da, db) * strip, ROWS)],
            dst_ref=whole.at[chunk, pl.ds(slot(db, da) * strip + ROWS, ROWS)],
            send_sem=send3.at[chunk, slot(da, db)],
            recv_sem=recv3.at[chunk, slot(da, db)],
            device_id=device(0, 0, 1),
            device_id_type=MESH,
        )

    def first_sum(chunk, da):
        rows = SIDE * strip
        return pltpu.make_async_remote_copy(
            src_ref=ladder.at[chunk, pl.ds(da * rows, rows)],
            dst_ref=level1.at[chunk, da - 1],
            send_sem=send4.at[chunk, da - 1],
            recv_sem=recv4.at[chunk, da - 1],
            device_id=device(-da, 0),
            device_id_type=MESH,
        )

    def second_sum(chunk, db):
        return pltpu.make_async_remote_copy(
            src_ref=summed.at[chunk, pl.ds(db * strip, strip)],
            dst_ref=level2.at[chunk, db - 1],
            send_sem=send5.at[chunk, db - 1],
            recv_sem=recv5.at[chunk, db - 1],
            device_id=device(0, -db),
            device_id_type=MESH,
        )

    barrier = pltpu.get_barrier_semaphore()
    for da, db in SHIFTS:
        for flip in range(2):
            if (da, db, flip) != (0, 0, 0):
                pl.semaphore_signal(
                    barrier, inc=1, device_id=device(da, db, flip), device_id_type=MESH
                )
    pl.semaphore_wait(barrier, 2 * SLABS - 1)

    for chunk in range(CHUNKS):
        for da, db in SHIFTS:
            for flip in range(2):
                spread(chunk, da, db, flip).start()

    v_copy.wait()
    tile = 64

    @pl.loop(0, v_raw.shape[0] // tile)
    def _(n):
        at = pl.ds(pl.multiple_of(n * tile, tile), tile)
        value = v_raw[at, :]
        high = value.astype(jnp.bfloat16)
        v_hi[at, :] = high
        v_lo[at, :] = (value - high.astype(jnp.float32)).astype(jnp.bfloat16)

    for chunk in range(CHUNKS):
        for da, db in SHIFTS:
            for flip in range(2):
                if (da, db, flip) == (0, 0, 0):
                    spread(chunk, 0, 0, 0).wait()
                else:
                    spread_arrival(chunk, da, db, flip).wait_recv()
        for da, db in SHIFTS:
            first = slab_at(da, db) * owned
            for k in range(owned):
                piece = parts[chunk][source_ref[first + k]]
                if (da, db) == (0, 0):
                    whole[chunk, 0:ROWS, k * BLK:(k + 1) * BLK] = piece
                else:
                    send_buf[chunk, slot(da, db), :, k * BLK:(k + 1) * BLK] = piece
            if (da, db) != (0, 0):
                collect(chunk, da, db).start()
            else:
                share(chunk, 0, 0).start()

    def exchange(chunk):
        for da, db in SHIFTS:
            if (da, db) != (0, 0):
                collect(chunk, da, db).wait_recv()
                share(chunk, da, db).start()

    def multiply(chunk):
        for da, db in SHIFTS:
            share(chunk, da, db).wait_recv()
        m = whole.shape[1]

        @pl.loop(0, m // 32)
        def _(n):
            at = pl.ds(pl.multiple_of(n * 32, 32), 32)
            value = whole[chunk, at, :]
            high = value.astype(jnp.bfloat16)
            split[at, :] = high
            split[pl.ds(pl.multiple_of(m + n * 32, 32), 32), :] = (
                value - high.astype(jnp.float32)
            ).astype(jnp.bfloat16)

        width = 256

        @pl.loop(0, v_hi.shape[0] // width)
        def _(n):
            at = pl.ds(pl.multiple_of(n * width, width), width)
            dims = (((1,), (1,)), ((), ()))
            both = lax.dot_general(
                split[...], v_hi[at, :], dims, preferred_element_type=jnp.float32
            )
            low = lax.dot_general(
                split[0:m, :], v_lo[at, :], dims, preferred_element_type=jnp.float32
            )
            ladder[chunk, :, at] = both[0:m] + (both[m:] + low)

        for da in range(1, SIDE):
            first_sum(chunk, da).start()

    def add_first(chunk):
        rows = SIDE * strip
        for da in range(1, SIDE):
            first_sum(chunk, da).wait_recv()
        summed[chunk] = (ladder[chunk, 0:rows, :] + level1[chunk, 0]) + (
            level1[chunk, 1] + level1[chunk, 2]
        )
        for db in range(1, SIDE):
            second_sum(chunk, db).start()

    def add_second(chunk):
        for db in range(1, SIDE):
            second_sum(chunk, db).wait_recv()
        total = (summed[chunk, 0:strip, :] + level2[chunk, 0]) + (
            level2[chunk, 1] + level2[chunk, 2]
        )
        for part in range(2):
            at = pl.ds(
                pl.multiple_of(((core + part) % 2) * strip + chunk * ROWS, ROWS), ROWS
            )
            out_ref[at, :] = r_ref[at, :] + total[part * ROWS:(part + 1) * ROWS]

    exchange(0)
    multiply(0)
    exchange(1)
    add_first(0)
    multiply(1)
    add_second(0)
    add_first(1)
    add_second(1)

    for chunk in range(CHUNKS):
        for da, db in SHIFTS:
            for flip in range(2):
                if (da, db, flip) != (0, 0, 0):
                    spread(chunk, da, db, flip).wait_send()
            if (da, db) != (0, 0):
                collect(chunk, da, db).wait_send()
            share(chunk, da, db).wait_send()
        for d in range(1, SIDE):
            first_sum(chunk, d).wait_send()
            second_sum(chunk, d).wait_send()


def per_device(t2_stored, v_slab, block_source, r_in):
    blocks = block_source.shape[0]
    tiles = t2_stored.reshape(t2_stored.shape[0] // ROWS, ROWS, -1, BLK).transpose(0, 2, 1, 3)
    ab, cd = v_slab.shape
    strip = CHUNKS * ROWS
    rows = SLABS * strip
    f32, bf16 = jnp.float32, jnp.bfloat16
    dma = pltpu.SemaphoreType.DMA
    return pl.pallas_call(
        kernel,
        out_shape=jax.ShapeDtypeStruct(r_in.shape, f32),
        in_specs=[
            pl.BlockSpec(memory_space=pltpu.SMEM),
            pl.BlockSpec(memory_space=pl.ANY),
            pl.BlockSpec(memory_space=pl.ANY),
            pl.BlockSpec(memory_space=pltpu.VMEM),
        ],
        out_specs=pl.BlockSpec(memory_space=pltpu.VMEM),
        scratch_shapes=[
            pltpu.VMEM((ab, cd), f32),
            pltpu.VMEM((ab, cd), bf16),
            pltpu.VMEM((ab, cd), bf16),
            pltpu.VMEM((blocks, ROWS, BLK), f32),
            pltpu.VMEM((blocks, ROWS, BLK), f32),
            pltpu.VMEM((CHUNKS, SLABS, ROWS, cd), f32),
            pltpu.VMEM((CHUNKS, rows, cd), f32),
            pltpu.VMEM((2 * rows, cd), bf16),
            pltpu.VMEM((CHUNKS, rows, ab), f32),
            pltpu.VMEM((CHUNKS, SIDE - 1, SIDE * strip, ab), f32),
            pltpu.VMEM((CHUNKS, SIDE * strip, ab), f32),
            pltpu.VMEM((CHUNKS, SIDE - 1, strip, ab), f32),
            dma,
            dma((CHUNKS,)),
            dma((CHUNKS, 2 * SLABS)),
            dma((CHUNKS, 2 * SLABS)),
            dma((CHUNKS, SLABS)),
            dma((CHUNKS, SLABS)),
            dma((CHUNKS, SLABS)),
            dma((CHUNKS, SLABS)),
            dma((CHUNKS, SIDE - 1)),
            dma((CHUNKS, SIDE - 1)),
            dma((CHUNKS, SIDE - 1)),
            dma((CHUNKS, SIDE - 1)),
        ],
        compiler_params=pltpu.CompilerParams(
            collective_id=1, has_side_effects=True, vmem_limit_bytes=60 * 1024 * 1024
        ),
        name="ladder",
    )(block_source, tiles, v_slab, r_in)


def solution(mesh):
    in_specs = (P("row", ("slab", "rep")), P("rep", "slab"), P(), P(("row", "slab"), "rep"))
    out_specs = P(("row", "slab"), "rep")
    return jax.shard_map(
        per_device, mesh=mesh, in_specs=in_specs, out_specs=out_specs, check_vma=False
    )
```

```python
import jax
import jax.numpy as jnp
from jax import lax
from jax.experimental import pallas as pl
from jax.experimental.pallas import tpu as pltpu
from jax.sharding import PartitionSpec as P

BLK = 128
SIDE = 4
SLABS = 16
CHUNKS = 2
ROWS = 8
MESH = pl.DeviceIdType.MESH


SHIFTS = (2, 1, 3)
WIDTH = 256


def kernel(
    place_ref, t2_ref, v_ref, out_ref,
    v_raw, v_hi, v_lo, relay1, part_a, part_b, send_buf, relay2, whole, split,
    ladder, level1, summed, level2,
    v_sem, own_sem, send1, recv1, send2, recv2, send3, recv3, send4, recv4,
    send5, recv5, send6, recv6, send7, recv7,
):
    row = lax.axis_index("row")
    slab = lax.axis_index("slab")
    core = lax.axis_index("rep")
    x, y = slab // SIDE, slab % SIDE
    a = x + core * (y - x)
    b = y + core * (x - y)
    stored = t2_ref.shape[3]
    owned = v_ref.shape[1] // BLK
    ab = v_ref.shape[0]
    strip = 2 * ROWS
    group = SIDE * strip
    parts = (part_a, part_b)

    def slab_at(aa, bb):
        xx, yy = aa + core * (bb - aa), bb + core * (aa - bb)
        return xx * SIDE + yy

    def device(da, db, flip=0):
        return (row, slab_at((a + da + SIDE) % SIDE, (b + db + SIDE) % SIDE), (core + flip) % 2)

    def remote(src, dst, send_sem, recv_sem, da, db, flip=0):
        return pltpu.make_async_remote_copy(
            src_ref=src,
            dst_ref=dst,
            send_sem=send_sem,
            recv_sem=recv_sem,
            device_id=device(da, db, flip),
            device_id_type=MESH,
        )

    def spread_a(chunk, da, to_b):
        src = t2_ref.at[slab_at((a + da) % SIDE, to_b), chunk]
        dst = relay1.at[chunk, to_b, :, pl.ds(a * stored, stored)]
        if da == 0:
            return pltpu.make_async_copy(src, dst, own_sem.at[chunk, to_b])
        return remote(
            src, dst, send1.at[chunk, da - 1, to_b], recv1.at[chunk, da - 1, to_b], da, 0
        )

    def spread_a_arrival(chunk, da, to_b):
        here = relay1.at[chunk, to_b, :, pl.ds(((a - da + SIDE) % SIDE) * stored, stored)]
        return remote(
            here, here, send1.at[chunk, da - 1, to_b], recv1.at[chunk, da - 1, to_b], da, 0
        )

    def spread_b(chunk, db, flip):
        src = relay1.at[chunk, (b + db) % SIDE, (core + flip) % 2]
        n = SIDE * stored
        dst = parts[chunk].at[pl.ds((core * SIDE + b) * n, n)]
        if (db, flip) == (0, 0):
            return pltpu.make_async_copy(src, dst, own_sem.at[chunk, SIDE])
        return remote(
            src, dst, send2.at[chunk, db, flip], recv2.at[chunk, db, flip], 0, db, flip
        )

    def spread_b_arrival(chunk, db, flip):
        n = SIDE * stored
        from_b = ((a if flip else b) - db + SIDE) % SIDE
        here = parts[chunk].at[pl.ds(((core + flip) % 2 * SIDE + from_b) * n, n)]
        return remote(
            here, here, send2.at[chunk, db, flip], recv2.at[chunk, db, flip], 0, db, flip
        )

    def collect_a(chunk, da):
        return remote(
            send_buf.at[chunk, da - 1],
            relay2.at[chunk, :, da],
            send3.at[chunk, da - 1],
            recv3.at[chunk, da - 1],
            da,
            0,
        )

    def collect_b(chunk, db):
        src = relay2.at[chunk, (b + db) % SIDE]
        dst = whole.at[chunk, :, db, 0]
        if db == 0:
            return pltpu.make_async_copy(src, dst, own_sem.at[chunk, SIDE + 1])
        return remote(src, dst, send4.at[chunk, db - 1], recv4.at[chunk, db - 1], 0, db)

    def share(chunk, db):
        src = relay2.at[chunk, b] if db == 0 else whole.at[chunk, :, db, 0]
        return remote(
            src, whole.at[chunk, db, :, 1], send5.at[chunk, db], recv5.at[chunk, db], 0, 0, 1
        )

    def first_sum(chunk, da, n):
        cols = pl.ds(n * WIDTH, WIDTH)
        return remote(
            ladder.at[chunk, da, :, cols],
            level1.at[chunk, da - 1, :, cols],
            send6.at[chunk, da - 1, n],
            recv6.at[chunk, da - 1, n],
            -da,
            0,
        )

    def second_sum(chunk, db):
        return remote(
            summed.at[chunk, pl.ds(db * strip, strip)],
            level2.at[chunk, db - 1],
            send7.at[chunk, db - 1],
            recv7.at[chunk, db - 1],
            0,
            -db,
        )

    def start_spread_a(chunk):
        for da in SHIFTS + (0,):
            for to_b in range(SIDE):
                spread_a(chunk, da, to_b).start()

    def start_spread_b(chunk):
        for to_b in range(SIDE):
            spread_a(chunk, 0, to_b).wait()
            for da in SHIFTS:
                spread_a_arrival(chunk, da, to_b).wait_recv()
        for db in SHIFTS + (0,):
            for flip in range(2):
                spread_b(chunk, db, flip).start()

    def start_collect_a(chunk):
        for db in SHIFTS + (0,):
            for flip in range(2):
                if (db, flip) == (0, 0):
                    spread_b(chunk, 0, 0).wait()
                else:
                    spread_b_arrival(chunk, db, flip).wait_recv()
        for da in SHIFTS + (0,):
            for to_b in range(SIDE):
                first = slab_at((a + da) % SIDE, to_b) * owned
                for k in range(owned):
                    piece = parts[chunk][place_ref[first + k]]
                    cols = slice(k * BLK, (k + 1) * BLK)
                    if da == 0:
                        relay2[chunk, to_b, 0, :, cols] = piece
                    else:
                        send_buf[chunk, da - 1, to_b, :, cols] = piece
            if da:
                collect_a(chunk, da).start()

    def start_collect_b(chunk):
        for da in SHIFTS:
            collect_a(chunk, da).wait_recv()
        for db in SHIFTS + (0,):
            collect_b(chunk, db).start()
        share(chunk, 0).start()

    def start_share(chunk):
        for db in SHIFTS:
            collect_b(chunk, db).wait_recv()
            share(chunk, db).start()
        collect_b(chunk, 0).wait()

    def multiply(chunk):
        for db in (0,) + SHIFTS:
            share(chunk, db).wait_recv()
        m = SIDE * group

        @pl.loop(0, SIDE)
        def _(n):
            value = whole[chunk, n].reshape(group, v_hi.shape[0])
            high = value.astype(jnp.bfloat16)
            at = pl.multiple_of(n * group, group)
            split[pl.ds(at, group), :] = high
            split[pl.ds(pl.multiple_of(m + at, group), group), :] = (
                value - high.astype(jnp.float32)
            ).astype(jnp.bfloat16)

        for n in range(ab // WIDTH):
            cols = slice(n * WIDTH, (n + 1) * WIDTH)
            dims = (((1,), (0,)), ((), ()))
            both = lax.dot_general(
                split[...], v_hi[:, cols], dims, preferred_element_type=jnp.float32
            )
            low = lax.dot_general(
                split[0:m, :], v_lo[:, cols], dims, preferred_element_type=jnp.float32
            )
            ladder[chunk, :, :, cols] = (both[0:m] + (both[m:] + low)).reshape(
                SIDE, group, WIDTH
            )
            for da in SHIFTS:
                first_sum(chunk, da, n).start()

    def add_first(chunk):
        for n in range(ab // WIDTH):
            for da in SHIFTS:
                first_sum(chunk, da, n).wait_recv()
            cols = slice(n * WIDTH, (n + 1) * WIDTH)
            summed[chunk, :, cols] = (ladder[chunk, 0, :, cols] + level1[chunk, 0, :, cols]) + (
                level1[chunk, 1, :, cols] + level1[chunk, 2, :, cols]
            )
        for db in SHIFTS:
            second_sum(chunk, db).start()

    def add_second(chunk):
        for db in SHIFTS:
            second_sum(chunk, db).wait_recv()
        total = (summed[chunk, 0:strip, :] + level2[chunk, 0]) + (
            level2[chunk, 1] + level2[chunk, 2]
        )
        for part in range(2):
            at = pl.ds(
                pl.multiple_of(chunk * strip + ((core + part) % 2) * ROWS, ROWS), ROWS
            )
            out_ref[at, :] = total[part * ROWS:(part + 1) * ROWS]

    v_copy = pltpu.make_async_copy(v_ref, v_raw, v_sem)
    v_copy.start()

    barrier = pltpu.get_barrier_semaphore()
    greeted = [(d, 0, 0) for d in SHIFTS] + [(0, d, f) for d in SHIFTS for f in range(2)]
    greeted += [(0, 0, 1)] + [(d, 0, 1) for d in SHIFTS]
    for da, db, flip in greeted:
        pl.semaphore_signal(barrier, inc=1, device_id=device(da, db, flip), device_id_type=MESH)
    pl.semaphore_wait(barrier, len(greeted))

    start_spread_a(0)

    v_copy.wait()
    tile = 256

    @pl.loop(0, v_raw.shape[1] // tile)
    def _(n):
        cd = pl.ds(pl.multiple_of(n * tile, tile), tile)
        for m in range(0, v_raw.shape[0], tile):
            value = v_raw[m:m + tile, cd]
            high = value.astype(jnp.bfloat16)
            low = (value - high.astype(jnp.float32)).astype(jnp.bfloat16)
            v_hi[cd, m:m + tile] = high.T
            v_lo[cd, m:m + tile] = low.T

    start_spread_a(1)
    for step in (start_spread_b, start_collect_a, start_collect_b):
        for chunk in range(CHUNKS):
            step(chunk)
    start_share(0)
    multiply(0)
    start_share(1)
    add_first(0)
    multiply(1)
    add_second(0)
    add_first(1)
    add_second(1)

    for chunk in range(CHUNKS):
        for d in SHIFTS:
            for to_b in range(SIDE):
                spread_a(chunk, d, to_b).wait_send()
            for flip in range(2):
                spread_b(chunk, d, flip).wait_send()
            collect_a(chunk, d).wait_send()
            collect_b(chunk, d).wait_send()
            share(chunk, d).wait_send()
            for n in range(ab // WIDTH):
                first_sum(chunk, d, n).wait_send()
            second_sum(chunk, d).wait_send()
        spread_b(chunk, 0, 1).wait_send()
        share(chunk, 0).wait_send()


def per_device(t2_stored, v_slab, block_source, r_in):
    ab, cd = v_slab.shape
    blocks = block_source.shape[0]
    stored = t2_stored.shape[1] // BLK
    owned = cd // BLK
    tiles = t2_stored.reshape(-1, ROWS, stored, BLK).transpose(0, 2, 1, 3)
    tiles = tiles.reshape(SLABS, CHUNKS, 2, stored, ROWS, BLK)
    holder = block_source // stored
    core = holder % 2
    x, y = holder // (2 * SIDE), holder // 2 % SIDE
    a, b = jnp.where(core == 0, x, y), jnp.where(core == 0, y, x)
    place = ((core * SIDE + b) * SIDE + a) * stored + block_source % stored
    strip = 2 * ROWS
    group = SIDE * strip
    f32, bf16 = jnp.float32, jnp.bfloat16
    dma = pltpu.SemaphoreType.DMA
    widths = ab // WIDTH
    ladder = pl.pallas_call(
        kernel,
        out_shape=jax.ShapeDtypeStruct(r_in.shape, f32),
        in_specs=[
            pl.BlockSpec(memory_space=pltpu.SMEM),
            pl.BlockSpec(memory_space=pl.ANY),
            pl.BlockSpec(memory_space=pl.ANY),
        ],
        out_specs=pl.BlockSpec(memory_space=pltpu.VMEM),
        scratch_shapes=[
            pltpu.VMEM((ab, cd), f32),
            pltpu.VMEM((cd, ab), bf16),
            pltpu.VMEM((cd, ab), bf16),
            pltpu.VMEM((CHUNKS, SIDE, 2, SIDE * stored, ROWS, BLK), f32),
            pltpu.VMEM((blocks, ROWS, BLK), f32),
            pltpu.VMEM((blocks, ROWS, BLK), f32),
            pltpu.VMEM((CHUNKS, SIDE - 1, SIDE, ROWS, cd), f32),
            pltpu.VMEM((CHUNKS, SIDE, SIDE, ROWS, cd), f32),
            pltpu.VMEM((CHUNKS, SIDE, SIDE, 2, ROWS, cd), f32),
            pltpu.VMEM((2 * SIDE * group, cd), bf16),
            pltpu.VMEM((CHUNKS, SIDE, group, ab), f32),
            pltpu.VMEM((CHUNKS, SIDE - 1, group, ab), f32),
            pltpu.VMEM((CHUNKS, group, ab), f32),
            pltpu.VMEM((CHUNKS, SIDE - 1, strip, ab), f32),
            dma,
            dma((CHUNKS, SIDE + 2)),
            dma((CHUNKS, SIDE - 1, SIDE)),
            dma((CHUNKS, SIDE - 1, SIDE)),
            dma((CHUNKS, SIDE, 2)),
            dma((CHUNKS, SIDE, 2)),
            dma((CHUNKS, SIDE - 1)),
            dma((CHUNKS, SIDE - 1)),
            dma((CHUNKS, SIDE - 1)),
            dma((CHUNKS, SIDE - 1)),
            dma((CHUNKS, SIDE)),
            dma((CHUNKS, SIDE)),
            dma((CHUNKS, SIDE - 1, widths)),
            dma((CHUNKS, SIDE - 1, widths)),
            dma((CHUNKS, SIDE - 1)),
            dma((CHUNKS, SIDE - 1)),
        ],
        compiler_params=pltpu.CompilerParams(
            collective_id=1, has_side_effects=True, vmem_limit_bytes=60 * 1024 * 1024
        ),
        name="ladder",
    )(place, tiles, v_slab)
    return r_in + ladder


def solution(mesh):
    in_specs = (P("row", ("slab", "rep")), P("rep", "slab"), P(), P(("row", "slab"), "rep"))
    out_specs = P(("row", "slab"), "rep")
    return jax.shard_map(
        per_device, mesh=mesh, in_specs=in_specs, out_specs=out_specs, check_vma=False
    )
```

```python
import jax
import jax.numpy as jnp
from jax import lax
from jax.experimental import pallas as pl
from jax.experimental.pallas import tpu as pltpu
from jax.sharding import PartitionSpec as P

BLK = 128
SIDE = 4
SLABS = 16
CHUNKS = 2
ROWS = 8
MESH = pl.DeviceIdType.MESH


SHIFTS = (2, 1, 3)
ARRIVALS = (2, 1, 3)
SPREAD = sorted(
    [(da, db) for da in range(SIDE) for db in range(SIDE)],
    key=lambda d: -sum(min(n, SIDE - n) for n in d),
)
GROUPS = (2, 1, 3, 0)


def kernel(
    source_ref, t2_ref, v_ref, out_ref,
    v_raw, v_hi, v_lo, part_a, part_b, send_buf, relay2, whole, split,
    ladder, level1, summed, level2,
    v_sem, own_sem, send1, recv1, send3, recv3, send4, recv4,
    send5, recv5, send6, recv6, send7, recv7,
):
    row = lax.axis_index("row")
    slab = lax.axis_index("slab")
    core = lax.axis_index("rep")
    x, y = slab // SIDE, slab % SIDE
    a = x + core * (y - x)
    b = y + core * (x - y)
    stored = t2_ref.shape[3]
    owned = v_ref.shape[1] // BLK
    group = SIDE * ROWS
    parts = (part_a, part_b)

    def slab_at(aa, bb):
        xx, yy = aa + core * (bb - aa), bb + core * (aa - bb)
        return xx * SIDE + yy

    def device(da, db, flip=0):
        return (row, slab_at((a + da + SIDE) % SIDE, (b + db + SIDE) % SIDE), (core + flip) % 2)

    def remote(src, dst, send_sem, recv_sem, da, db, flip=0):
        return pltpu.make_async_remote_copy(
            src_ref=src,
            dst_ref=dst,
            send_sem=send_sem,
            recv_sem=recv_sem,
            device_id=device(da, db, flip),
            device_id_type=MESH,
        )

    def spread(chunk, da, db, flip):
        to_slab = slab_at((a + da) % SIDE, (b + db) % SIDE)
        src = t2_ref.at[to_slab, chunk, (core + flip) % 2]
        dst = parts[chunk].at[pl.ds((slab * 2 + core) * stored, stored)]
        if (da, db, flip) == (0, 0, 0):
            return pltpu.make_async_copy(src, dst, own_sem.at[chunk, 0])
        n = (da * SIDE + db) * 2 + flip
        return remote(src, dst, send1.at[chunk, n], recv1.at[chunk, n], da, db, flip)

    def spread_arrival(chunk, da, db, flip):
        ea, eb = (db, da) if flip else (da, db)
        from_slab = slab_at((a - ea + SIDE) % SIDE, (b - eb + SIDE) % SIDE)
        here = parts[chunk].at[pl.ds((from_slab * 2 + (core + flip) % 2) * stored, stored)]
        n = (da * SIDE + db) * 2 + flip
        return remote(here, here, send1.at[chunk, n], recv1.at[chunk, n], da, db, flip)

    def collect_a(chunk, da):
        return remote(
            send_buf.at[chunk, da - 1],
            relay2.at[chunk, :, da],
            send3.at[chunk, da - 1],
            recv3.at[chunk, da - 1],
            da,
            0,
        )

    def collect_b(chunk, da, db):
        src = relay2.at[chunk, (b + db) % SIDE, da]
        dst = whole.at[chunk, 0, da, db]
        if db == 0:
            return pltpu.make_async_copy(src, dst, own_sem.at[chunk, SIDE + da])
        n = db - 1
        return remote(src, dst, send4.at[chunk, da, n], recv4.at[chunk, da, n], 0, db)

    def share(chunk, da, db):
        src = relay2.at[chunk, b, da] if db == 0 else whole.at[chunk, 0, da, db]
        dst = whole.at[chunk, 1, da, db]
        return remote(src, dst, send5.at[chunk, da, db], recv5.at[chunk, da, db], 0, 0, 1)

    def first_sum(chunk, part, d):
        return remote(
            ladder.at[chunk, part, d],
            level1.at[chunk, part, d - 1],
            send6.at[chunk, part, d - 1],
            recv6.at[chunk, part, d - 1],
            *((-d, 0), (0, -d))[part],
        )

    def second_sum(chunk, part, d):
        return remote(
            summed.at[chunk, part, pl.ds(d * ROWS, ROWS)],
            level2.at[chunk, part, d - 1],
            send7.at[chunk, part, d - 1],
            recv7.at[chunk, part, d - 1],
            *((0, -d), (-d, 0))[part],
        )

    def start_spread(chunk):
        for da, db in SPREAD:
            for flip in range(2):
                spread(chunk, da, db, flip).start()

    def forward_blocks(chunk, da):
        for db in SHIFTS + (0,):
            collect_b(chunk, da, db).start()
        share(chunk, da, 0).start()

    def start_collect(chunk):
        for da, db in SPREAD:
            for flip in range(2):
                if (da, db, flip) == (0, 0, 0):
                    spread(chunk, 0, 0, 0).wait()
                else:
                    spread_arrival(chunk, da, db, flip).wait_recv()
        for da in SHIFTS + (0,):
            for to_b in range(SIDE):
                first = slab_at((a + da) % SIDE, to_b) * owned
                for k in range(owned):
                    piece = parts[chunk][source_ref[first + k]]
                    cols = slice(k * BLK, (k + 1) * BLK)
                    if da == 0:
                        relay2[chunk, to_b, 0, :, cols] = piece
                    else:
                        send_buf[chunk, da - 1, to_b, :, cols] = piece
            if da:
                collect_a(chunk, da).start()
        forward_blocks(chunk, 0)

    def forward_collect(chunk):
        for da in ARRIVALS:
            collect_a(chunk, da).wait_recv()
            forward_blocks(chunk, da)

    def exchange(chunk, da):
        for db in ARRIVALS:
            collect_b(chunk, da, db).wait_recv()
            share(chunk, da, db).start()

    def multiply(chunk, da):
        collect_b(chunk, da, 0).wait()
        for db in range(SIDE):
            share(chunk, da, db).wait_recv()
        value = whole[chunk, :, da].reshape(2 * group, v_hi.shape[0])
        high = value.astype(jnp.bfloat16)
        split[0:2 * group, :] = high
        split[2 * group:, :] = (value - high.astype(jnp.float32)).astype(jnp.bfloat16)
        dims = (((1,), (0,)), ((), ()))
        both = lax.dot_general(
            split[...], v_hi[...], dims, preferred_element_type=jnp.float32
        )
        low = lax.dot_general(
            split[0:2 * group, :], v_lo[...], dims, preferred_element_type=jnp.float32
        )
        total = both[0:2 * group] + (both[2 * group:] + low)
        for part in range(2):
            ladder[chunk, part, da] = total[part * group:(part + 1) * group]
            if da:
                first_sum(chunk, part, da).start()

    def add_first(chunk):
        for part in range(2):
            for d in ARRIVALS:
                first_sum(chunk, part, d).wait_recv()
            summed[chunk, part] = (ladder[chunk, part, 0] + level1[chunk, part, 0]) + (
                level1[chunk, part, 1] + level1[chunk, part, 2]
            )
            for d in SHIFTS:
                second_sum(chunk, part, d).start()

    def add_second(chunk):
        for part in range(2):
            for d in SHIFTS:
                second_sum(chunk, part, d).wait_recv()
            at = pl.ds(
                pl.multiple_of((chunk * 2 + (core + part) % 2) * ROWS, ROWS), ROWS
            )
            out_ref[at, :] = (summed[chunk, part, 0:ROWS, :] + level2[chunk, part, 0]) + (
                level2[chunk, part, 1] + level2[chunk, part, 2]
            )

    v_copy = pltpu.make_async_copy(v_ref, v_raw, v_sem)
    v_copy.start()

    barrier = pltpu.get_barrier_semaphore()
    for da, db in SPREAD:
        for flip in range(2):
            if (da, db, flip) != (0, 0, 0):
                pl.semaphore_signal(
                    barrier, inc=1, device_id=device(da, db, flip), device_id_type=MESH
                )
    pl.semaphore_wait(barrier, 2 * SLABS - 1)

    start_spread(0)
    start_spread(1)

    v_copy.wait()
    tile = 256

    @pl.loop(0, v_raw.shape[1] // tile)
    def _(n):
        cd = pl.ds(pl.multiple_of(n * tile, tile), tile)
        for m in range(0, v_raw.shape[0], tile):
            value = v_raw[m:m + tile, cd]
            high = value.astype(jnp.bfloat16)
            low = (value - high.astype(jnp.float32)).astype(jnp.bfloat16)
            v_hi[cd, m:m + tile] = high.T
            v_lo[cd, m:m + tile] = low.T

    for chunk in range(CHUNKS):
        start_collect(chunk)
    for chunk in range(CHUNKS):
        forward_collect(chunk)
    ahead = None
    for da in GROUPS:
        for chunk in range(CHUNKS):
            exchange(chunk, da)
            if ahead:
                multiply(*ahead)
            ahead = (chunk, da)
    multiply(*ahead)
    for chunk in range(CHUNKS):
        add_first(chunk)
    for chunk in range(CHUNKS):
        add_second(chunk)

    for chunk in range(CHUNKS):
        for da in range(SIDE):
            for db in range(SIDE):
                for flip in range(2):
                    if (da, db, flip) != (0, 0, 0):
                        spread(chunk, da, db, flip).wait_send()
                if db:
                    collect_b(chunk, da, db).wait_send()
                share(chunk, da, db).wait_send()
        for d in SHIFTS:
            collect_a(chunk, d).wait_send()
            for part in range(2):
                first_sum(chunk, part, d).wait_send()
                second_sum(chunk, part, d).wait_send()


def per_device(t2_stored, v_slab, block_source, r_in):
    ab, cd = v_slab.shape
    blocks = block_source.shape[0]
    stored = t2_stored.shape[1] // BLK
    owned = cd // BLK
    tiles = t2_stored.reshape(-1, ROWS, stored, BLK).transpose(0, 2, 1, 3)
    tiles = tiles.reshape(SLABS, CHUNKS, 2, stored, ROWS, BLK)
    group = SIDE * ROWS
    f32, bf16 = jnp.float32, jnp.bfloat16
    dma = pltpu.SemaphoreType.DMA
    ladder = pl.pallas_call(
        kernel,
        out_shape=jax.ShapeDtypeStruct(r_in.shape, f32),
        in_specs=[
            pl.BlockSpec(memory_space=pltpu.SMEM),
            pl.BlockSpec(memory_space=pl.ANY),
            pl.BlockSpec(memory_space=pl.ANY),
        ],
        out_specs=pl.BlockSpec(memory_space=pltpu.VMEM),
        scratch_shapes=[
            pltpu.VMEM((ab, cd), f32),
            pltpu.VMEM((cd, ab), bf16),
            pltpu.VMEM((cd, ab), bf16),
            pltpu.VMEM((blocks, ROWS, BLK), f32),
            pltpu.VMEM((blocks, ROWS, BLK), f32),
            pltpu.VMEM((CHUNKS, SIDE - 1, SIDE, ROWS, cd), f32),
            pltpu.VMEM((CHUNKS, SIDE, SIDE, ROWS, cd), f32),
            pltpu.VMEM((CHUNKS, 2, SIDE, SIDE, ROWS, cd), f32),
            pltpu.VMEM((4 * group, cd), bf16),
            pltpu.VMEM((CHUNKS, 2, SIDE, group, ab), f32),
            pltpu.VMEM((CHUNKS, 2, SIDE - 1, group, ab), f32),
            pltpu.VMEM((CHUNKS, 2, group, ab), f32),
            pltpu.VMEM((CHUNKS, 2, SIDE - 1, ROWS, ab), f32),
            dma,
            dma((CHUNKS, 2 * SIDE)),
            dma((CHUNKS, 2 * SLABS)),
            dma((CHUNKS, 2 * SLABS)),
            dma((CHUNKS, SIDE - 1)),
            dma((CHUNKS, SIDE - 1)),
            dma((CHUNKS, SIDE, SIDE - 1)),
            dma((CHUNKS, SIDE, SIDE - 1)),
            dma((CHUNKS, SIDE, SIDE)),
            dma((CHUNKS, SIDE, SIDE)),
            dma((CHUNKS, 2, SIDE - 1)),
            dma((CHUNKS, 2, SIDE - 1)),
            dma((CHUNKS, 2, SIDE - 1)),
            dma((CHUNKS, 2, SIDE - 1)),
        ],
        compiler_params=pltpu.CompilerParams(
            collective_id=1, has_side_effects=True, vmem_limit_bytes=60 * 1024 * 1024
        ),
        name="ladder",
    )(block_source, tiles, v_slab)
    return r_in + ladder


def solution(mesh):
    in_specs = (P("row", ("slab", "rep")), P("rep", "slab"), P(), P(("row", "slab"), "rep"))
    out_specs = P(("row", "slab"), "rep")
    return jax.shard_map(
        per_device, mesh=mesh, in_specs=in_specs, out_specs=out_specs, check_vma=False
    )
```

```python
import jax
import jax.numpy as jnp
from jax import lax
from jax.experimental import pallas as pl
from jax.experimental.pallas import tpu as pltpu
from jax.sharding import PartitionSpec as P

BLK = 128
SIDE = 4
SLABS = 16
CHUNKS = 2
ROWS = 8
MESH = pl.DeviceIdType.MESH


SHIFTS = (2, 1, 3)
ARRIVALS = (2, 1, 3)
NEXT = (1, 3)
SPREAD = sorted(
    [(da, db) for da in range(SIDE) for db in range(SIDE)],
    key=lambda d: -sum(min(n, SIDE - n) for n in d),
)
GROUPS = (2, 1, 3, 0)


def kernel(
    source_ref, t2_ref, v_ref, out_ref,
    v_raw, v_hi, v_lo, part_a, part_b, send_buf, relay2, whole, split,
    ladder, folded, level1, summed, level2,
    v_sem, own_sem, send1, recv1, send3, recv3, send4, recv4,
    send5, recv5, send6, recv6, send7, recv7, send8, recv8,
):
    row = lax.axis_index("row")
    slab = lax.axis_index("slab")
    core = lax.axis_index("rep")
    x, y = slab // SIDE, slab % SIDE
    a = x + core * (y - x)
    b = y + core * (x - y)
    a_step = SIDE - core * (SIDE - 1)
    b_step = 1 + core * (SIDE - 1)
    to_a = [(a + d) & (SIDE - 1) for d in range(SIDE)]
    to_b = [(b + d) & (SIDE - 1) for d in range(SIDE)]
    a_term = [n * a_step for n in to_a]
    b_term = [n * b_step for n in to_b]
    b_all = [n * b_step for n in range(SIDE)]
    other = 1 - core
    stored = t2_ref.shape[3]
    owned = v_ref.shape[1] // BLK
    group = SIDE * ROWS
    half = group // 2
    parts = (part_a, part_b)

    def device(da, db, flip=0):
        return (row, a_term[da % SIDE] + b_term[db % SIDE], other if flip else core)

    def remote(src, dst, send_sem, recv_sem, da, db, flip=0):
        return pltpu.make_async_remote_copy(
            src_ref=src,
            dst_ref=dst,
            send_sem=send_sem,
            recv_sem=recv_sem,
            device_id=device(da, db, flip),
            device_id_type=MESH,
        )

    def spread(chunk, da, db, flip):
        src = t2_ref.at[a_term[da] + b_term[db], chunk, other if flip else core]
        dst = parts[chunk].at[pl.ds((slab * 2 + core) * stored, stored)]
        if (da, db, flip) == (0, 0, 0):
            return pltpu.make_async_copy(src, dst, own_sem.at[chunk, 0])
        n = (da * SIDE + db) * 2 + flip
        return remote(src, dst, send1.at[chunk, n], recv1.at[chunk, n], da, db, flip)

    def spread_arrival(chunk, da, db, flip):
        ea, eb = (db, da) if flip else (da, db)
        from_slab = a_term[-ea % SIDE] + b_term[-eb % SIDE]
        holder = from_slab * 2 + (other if flip else core)
        here = parts[chunk].at[pl.ds(holder * stored, stored)]
        n = (da * SIDE + db) * 2 + flip
        return remote(here, here, send1.at[chunk, n], recv1.at[chunk, n], da, db, flip)

    def collect_a(chunk, da):
        return remote(
            send_buf.at[chunk, da - 1],
            relay2.at[chunk, :, da],
            send3.at[chunk, da - 1],
            recv3.at[chunk, da - 1],
            da,
            0,
        )

    def collect_b(chunk, da, db):
        src = relay2.at[chunk, to_b[db], da]
        dst = whole.at[chunk, 0, da, db]
        if db == 0:
            return pltpu.make_async_copy(src, dst, own_sem.at[chunk, SIDE + da])
        n = db - 1
        return remote(src, dst, send4.at[chunk, da, n], recv4.at[chunk, da, n], 0, db)

    def share(chunk, da, db):
        src = relay2.at[chunk, b, da] if db == 0 else whole.at[chunk, 0, da, db]
        dst = whole.at[chunk, 1, da, db]
        return remote(src, dst, send5.at[chunk, da, db], recv5.at[chunk, da, db], 0, 0, 1)

    def fold(chunk, part, d):
        n = d // 2
        return remote(
            ladder.at[chunk, part, 2, pl.ds(n * half, half)],
            folded.at[chunk, part, n],
            send8.at[chunk, part, n],
            recv8.at[chunk, part, n],
            *((-d, 0), (0, -d))[part],
        )

    def first_sum(chunk, part, d):
        n = d // 2
        return remote(
            ladder.at[chunk, part, d],
            level1.at[chunk, part, n],
            send6.at[chunk, part, n],
            recv6.at[chunk, part, n],
            *((-d, 0), (0, -d))[part],
        )

    def second_sum(chunk, part, d):
        return remote(
            summed.at[chunk, part, pl.ds(d * ROWS, ROWS)],
            level2.at[chunk, part, d - 1],
            send7.at[chunk, part, d - 1],
            recv7.at[chunk, part, d - 1],
            *((0, -d), (-d, 0))[part],
        )

    def start_spread(chunk):
        for da, db in SPREAD:
            for flip in range(2):
                spread(chunk, da, db, flip).start()

    def forward_blocks(chunk, da):
        for db in SHIFTS + (0,):
            collect_b(chunk, da, db).start()
        share(chunk, da, 0).start()

    def start_collect(chunk):
        for da, db in SPREAD:
            for flip in range(2):
                if (da, db, flip) == (0, 0, 0):
                    spread(chunk, 0, 0, 0).wait()
                else:
                    spread_arrival(chunk, da, db, flip).wait_recv()
        for da in SHIFTS + (0,):
            for its_b in range(SIDE):
                first = (a_term[da] + b_all[its_b]) * owned
                for k in range(owned):
                    piece = parts[chunk][source_ref[first + k]]
                    cols = slice(k * BLK, (k + 1) * BLK)
                    if da == 0:
                        relay2[chunk, its_b, 0, :, cols] = piece
                    else:
                        send_buf[chunk, da - 1, its_b, :, cols] = piece
            if da:
                collect_a(chunk, da).start()
        forward_blocks(chunk, 0)

    def forward_collect(chunk):
        for da in ARRIVALS:
            collect_a(chunk, da).wait_recv()
            forward_blocks(chunk, da)

    def exchange(chunk, da):
        for db in ARRIVALS:
            collect_b(chunk, da, db).wait_recv()
            share(chunk, da, db).start()

    def multiply(chunk, da):
        collect_b(chunk, da, 0).wait()
        for db in range(SIDE):
            share(chunk, da, db).wait_recv()
        value = whole[chunk, :, da].reshape(2 * group, v_hi.shape[0])
        high = value.astype(jnp.bfloat16)
        split[0:2 * group, :] = high
        split[2 * group:, :] = (value - high.astype(jnp.float32)).astype(jnp.bfloat16)
        dims = (((1,), (0,)), ((), ()))
        both = lax.dot_general(
            split[...], v_hi[...], dims, preferred_element_type=jnp.float32
        )
        low = lax.dot_general(
            split[0:2 * group, :], v_lo[...], dims, preferred_element_type=jnp.float32
        )
        total = both[0:2 * group] + (both[2 * group:] + low)
        for part in range(2):
            at = part * group
            if da in NEXT:
                fold(chunk, part, da).wait_recv()
                n = da // 2
                near = slice(n * half, (n + 1) * half)
                far = slice((1 - n) * half, (2 - n) * half)
                ladder[chunk, part, da, near] = (
                    total[at + n * half:at + (n + 1) * half] + folded[chunk, part, n]
                )
                ladder[chunk, part, da, far] = total[at + (1 - n) * half:at + (2 - n) * half]
                first_sum(chunk, part, da).start()
            else:
                ladder[chunk, part, da] = total[at:at + group]
                if da:
                    for d in NEXT:
                        fold(chunk, part, d).start()

    def add_first(chunk):
        for part in range(2):
            for d in NEXT:
                first_sum(chunk, part, d).wait_recv()
            summed[chunk, part] = (
                ladder[chunk, part, 0] + level1[chunk, part, 0]
            ) + level1[chunk, part, 1]
            for d in SHIFTS:
                second_sum(chunk, part, d).start()

    def add_second(chunk):
        for part in range(2):
            for d in SHIFTS:
                second_sum(chunk, part, d).wait_recv()
            at = pl.ds(
                pl.multiple_of((chunk * 2 + (other if part else core)) * ROWS, ROWS), ROWS
            )
            out_ref[at, :] = (summed[chunk, part, 0:ROWS, :] + level2[chunk, part, 0]) + (
                level2[chunk, part, 1] + level2[chunk, part, 2]
            )

    v_copy = pltpu.make_async_copy(v_ref, v_raw, v_sem)
    v_copy.start()

    barrier = pltpu.get_barrier_semaphore()
    for da, db in SPREAD:
        for flip in range(2):
            if (da, db, flip) != (0, 0, 0):
                pl.semaphore_signal(
                    barrier, inc=1, device_id=device(da, db, flip), device_id_type=MESH
                )
    pl.semaphore_wait(barrier, 2 * SLABS - 1)

    start_spread(0)
    start_spread(1)

    v_copy.wait()
    tile = 256

    @pl.loop(0, v_raw.shape[1] // tile)
    def _(n):
        cd = pl.ds(pl.multiple_of(n * tile, tile), tile)
        for m in range(0, v_raw.shape[0], tile):
            value = v_raw[m:m + tile, cd]
            high = value.astype(jnp.bfloat16)
            low = (value - high.astype(jnp.float32)).astype(jnp.bfloat16)
            v_hi[cd, m:m + tile] = high.T
            v_lo[cd, m:m + tile] = low.T

    for chunk in range(CHUNKS):
        start_collect(chunk)
    for chunk in range(CHUNKS):
        forward_collect(chunk)
    ahead = None
    for da in GROUPS:
        for chunk in range(CHUNKS):
            exchange(chunk, da)
            if ahead:
                multiply(*ahead)
            ahead = (chunk, da)
    multiply(*ahead)
    for chunk in range(CHUNKS):
        add_first(chunk)
    for chunk in range(CHUNKS):
        add_second(chunk)

    for chunk in range(CHUNKS):
        for da in range(SIDE):
            for db in range(SIDE):
                for flip in range(2):
                    if (da, db, flip) != (0, 0, 0):
                        spread(chunk, da, db, flip).wait_send()
                if db:
                    collect_b(chunk, da, db).wait_send()
                share(chunk, da, db).wait_send()
        for d in SHIFTS:
            collect_a(chunk, d).wait_send()
            for part in range(2):
                second_sum(chunk, part, d).wait_send()
                if d in NEXT:
                    first_sum(chunk, part, d).wait_send()
                    fold(chunk, part, d).wait_send()


def per_device(t2_stored, v_slab, block_source, r_in):
    ab, cd = v_slab.shape
    blocks = block_source.shape[0]
    stored = t2_stored.shape[1] // BLK
    owned = cd // BLK
    tiles = t2_stored.reshape(-1, ROWS, stored, BLK).transpose(0, 2, 1, 3)
    tiles = tiles.reshape(SLABS, CHUNKS, 2, stored, ROWS, BLK)
    group = SIDE * ROWS
    f32, bf16 = jnp.float32, jnp.bfloat16
    dma = pltpu.SemaphoreType.DMA
    ladder = pl.pallas_call(
        kernel,
        out_shape=jax.ShapeDtypeStruct(r_in.shape, f32),
        in_specs=[
            pl.BlockSpec(memory_space=pltpu.SMEM),
            pl.BlockSpec(memory_space=pl.ANY),
            pl.BlockSpec(memory_space=pl.ANY),
        ],
        out_specs=pl.BlockSpec(memory_space=pltpu.VMEM),
        scratch_shapes=[
            pltpu.VMEM((ab, cd), f32),
            pltpu.VMEM((cd, ab), bf16),
            pltpu.VMEM((cd, ab), bf16),
            pltpu.VMEM((blocks, ROWS, BLK), f32),
            pltpu.VMEM((blocks, ROWS, BLK), f32),
            pltpu.VMEM((CHUNKS, SIDE - 1, SIDE, ROWS, cd), f32),
            pltpu.VMEM((CHUNKS, SIDE, SIDE, ROWS, cd), f32),
            pltpu.VMEM((CHUNKS, 2, SIDE, SIDE, ROWS, cd), f32),
            pltpu.VMEM((4 * group, cd), bf16),
            pltpu.VMEM((CHUNKS, 2, SIDE, group, ab), f32),
            pltpu.VMEM((CHUNKS, 2, 2, group // 2, ab), f32),
            pltpu.VMEM((CHUNKS, 2, 2, group, ab), f32),
            pltpu.VMEM((CHUNKS, 2, group, ab), f32),
            pltpu.VMEM((CHUNKS, 2, SIDE - 1, ROWS, ab), f32),
            dma,
            dma((CHUNKS, 2 * SIDE)),
            dma((CHUNKS, 2 * SLABS)),
            dma((CHUNKS, 2 * SLABS)),
            dma((CHUNKS, SIDE - 1)),
            dma((CHUNKS, SIDE - 1)),
            dma((CHUNKS, SIDE, SIDE - 1)),
            dma((CHUNKS, SIDE, SIDE - 1)),
            dma((CHUNKS, SIDE, SIDE)),
            dma((CHUNKS, SIDE, SIDE)),
            dma((CHUNKS, 2, 2)),
            dma((CHUNKS, 2, 2)),
            dma((CHUNKS, 2, SIDE - 1)),
            dma((CHUNKS, 2, SIDE - 1)),
            dma((CHUNKS, 2, 2)),
            dma((CHUNKS, 2, 2)),
        ],
        compiler_params=pltpu.CompilerParams(
            collective_id=1, has_side_effects=True, vmem_limit_bytes=60 * 1024 * 1024
        ),
        name="ladder",
    )(block_source, tiles, v_slab)
    return r_in + ladder


def solution(mesh):
    in_specs = (P("row", ("slab", "rep")), P("rep", "slab"), P(), P(("row", "slab"), "rep"))
    out_specs = P(("row", "slab"), "rep")
    return jax.shard_map(
        per_device, mesh=mesh, in_specs=in_specs, out_specs=out_specs, check_vma=False
    )
```

```python
import jax
import jax.numpy as jnp
from jax import lax
from jax.experimental import pallas as pl
from jax.experimental.pallas import tpu as pltpu
from jax.sharding import PartitionSpec as P

BLK = 128
SIDE = 4
SLABS = 16
CHUNKS = 2
ROWS = 8
MESH = pl.DeviceIdType.MESH


SHIFTS = (2, 1, 3)
ARRIVALS = (2, 1, 3)
NEXT = (1, 3)
SPREAD = sorted(
    [(da, db) for da in range(SIDE) for db in range(SIDE)],
    key=lambda d: -sum(min(n, SIDE - n) for n in d),
)
GROUPS = (2, 1, 3, 0)


def kernel(
    source_ref, t2_ref, v_ref, out_ref,
    v_raw, v_hi, v_lo, swapped, part_a, part_b, send_buf, relay2, whole, split,
    ladder, folded, level1, summed, level2,
    v_sem, swap_sem, own_sem, send1, recv1, send3, recv3, send4, recv4,
    send5, recv5, send6, recv6, send7, recv7, send8, recv8,
):
    row = lax.axis_index("row")
    slab = lax.axis_index("slab")
    core = lax.axis_index("rep")
    x, y = slab // SIDE, slab % SIDE
    a = x + core * (y - x)
    b = y + core * (x - y)
    a_step = SIDE - core * (SIDE - 1)
    b_step = 1 + core * (SIDE - 1)
    to_a = [(a + d) & (SIDE - 1) for d in range(SIDE)]
    to_b = [(b + d) & (SIDE - 1) for d in range(SIDE)]
    a_term = [n * a_step for n in to_a]
    b_term = [n * b_step for n in to_b]
    b_all = [n * b_step for n in range(SIDE)]
    other = 1 - core
    stored = t2_ref.shape[3]
    owned = v_ref.shape[1] // BLK
    group = SIDE * ROWS
    half = group // 2
    parts = (part_a, part_b)

    def device(da, db, flip=0):
        return (row, a_term[da % SIDE] + b_term[db % SIDE], other if flip else core)

    def remote(src, dst, send_sem, recv_sem, da, db, flip=0):
        return pltpu.make_async_remote_copy(
            src_ref=src,
            dst_ref=dst,
            send_sem=send_sem,
            recv_sem=recv_sem,
            device_id=device(da, db, flip),
            device_id_type=MESH,
        )

    def swap(chunk):
        return remote(
            t2_ref.at[:, chunk, other],
            swapped.at[chunk],
            swap_sem.at[2 * chunk],
            swap_sem.at[2 * chunk + 1],
            0,
            0,
            1,
        )

    def spread(chunk, da, db, flip):
        to_slab = a_term[da] + b_term[db]
        if flip:
            src = swapped.at[chunk, to_slab]
        else:
            src = t2_ref.at[to_slab, chunk, core]
        holder = slab * 2 + (other if flip else core)
        dst = parts[chunk].at[pl.ds(holder * stored, stored)]
        if (da, db) == (0, 0):
            return pltpu.make_async_copy(src, dst, swap_sem.at[4 + 2 * chunk + flip])
        n = (da * SIDE + db) * 2 + flip
        return remote(src, dst, send1.at[chunk, n], recv1.at[chunk, n], da, db)

    def spread_arrival(chunk, da, db, flip):
        holder = (a_term[-da % SIDE] + b_term[-db % SIDE]) * 2 + (other if flip else core)
        here = parts[chunk].at[pl.ds(holder * stored, stored)]
        n = (da * SIDE + db) * 2 + flip
        return remote(here, here, send1.at[chunk, n], recv1.at[chunk, n], da, db)

    def collect_a(chunk, da):
        return remote(
            send_buf.at[chunk, da - 1],
            relay2.at[chunk, :, da],
            send3.at[chunk, da - 1],
            recv3.at[chunk, da - 1],
            da,
            0,
        )

    def collect_b(chunk, da, db):
        src = relay2.at[chunk, to_b[db], da]
        dst = whole.at[chunk, 0, da, db]
        if db == 0:
            return pltpu.make_async_copy(src, dst, own_sem.at[chunk, SIDE + da])
        n = db - 1
        return remote(src, dst, send4.at[chunk, da, n], recv4.at[chunk, da, n], 0, db)

    def share(chunk, da, db):
        src = relay2.at[chunk, b, da] if db == 0 else whole.at[chunk, 0, da, db]
        dst = whole.at[chunk, 1, da, db]
        return remote(src, dst, send5.at[chunk, da, db], recv5.at[chunk, da, db], 0, 0, 1)

    def fold(chunk, part, d):
        n = d // 2
        return remote(
            ladder.at[chunk, part, 2, pl.ds(n * half, half)],
            folded.at[chunk, part, n],
            send8.at[chunk, part, n],
            recv8.at[chunk, part, n],
            *((-d, 0), (0, -d))[part],
        )

    def first_sum(chunk, part, d):
        n = d // 2
        return remote(
            ladder.at[chunk, part, d],
            level1.at[chunk, part, n],
            send6.at[chunk, part, n],
            recv6.at[chunk, part, n],
            *((-d, 0), (0, -d))[part],
        )

    def second_sum(chunk, part, d):
        return remote(
            summed.at[chunk, part, pl.ds(d * ROWS, ROWS)],
            level2.at[chunk, part, d - 1],
            send7.at[chunk, part, d - 1],
            recv7.at[chunk, part, d - 1],
            *((0, -d), (-d, 0))[part],
        )

    def start_spread(chunk, flip):
        for da, db in SPREAD:
            spread(chunk, da, db, flip).start()

    def forward_blocks(chunk, da):
        for db in SHIFTS + (0,):
            collect_b(chunk, da, db).start()
        share(chunk, da, 0).start()

    def start_collect(chunk):
        for da, db in SPREAD:
            for flip in range(2):
                if (da, db) == (0, 0):
                    spread(chunk, 0, 0, flip).wait()
                else:
                    spread_arrival(chunk, da, db, flip).wait_recv()
        for da in SHIFTS + (0,):
            for its_b in range(SIDE):
                first = (a_term[da] + b_all[its_b]) * owned
                for k in range(owned):
                    piece = parts[chunk][source_ref[first + k]]
                    cols = slice(k * BLK, (k + 1) * BLK)
                    if da == 0:
                        relay2[chunk, its_b, 0, :, cols] = piece
                    else:
                        send_buf[chunk, da - 1, its_b, :, cols] = piece
            if da:
                collect_a(chunk, da).start()
        forward_blocks(chunk, 0)

    def forward_collect(chunk):
        for da in ARRIVALS:
            collect_a(chunk, da).wait_recv()
            forward_blocks(chunk, da)

    def exchange(chunk, da):
        for db in ARRIVALS:
            collect_b(chunk, da, db).wait_recv()
            share(chunk, da, db).start()

    def multiply(chunk, da):
        collect_b(chunk, da, 0).wait()
        for db in range(SIDE):
            share(chunk, da, db).wait_recv()
        value = whole[chunk, :, da].reshape(2 * group, v_hi.shape[0])
        high = value.astype(jnp.bfloat16)
        split[0:2 * group, :] = high
        split[2 * group:, :] = (value - high.astype(jnp.float32)).astype(jnp.bfloat16)
        dims = (((1,), (0,)), ((), ()))
        both = lax.dot_general(
            split[...], v_hi[...], dims, preferred_element_type=jnp.float32
        )
        low = lax.dot_general(
            split[0:2 * group, :], v_lo[...], dims, preferred_element_type=jnp.float32
        )
        total = both[0:2 * group] + (both[2 * group:] + low)
        for part in range(2):
            at = part * group
            if da in NEXT:
                fold(chunk, part, da).wait_recv()
                n = da // 2
                near = slice(n * half, (n + 1) * half)
                far = slice((1 - n) * half, (2 - n) * half)
                ladder[chunk, part, da, near] = (
                    total[at + n * half:at + (n + 1) * half] + folded[chunk, part, n]
                )
                ladder[chunk, part, da, far] = total[at + (1 - n) * half:at + (2 - n) * half]
                first_sum(chunk, part, da).start()
            else:
                ladder[chunk, part, da] = total[at:at + group]
                if da:
                    for d in NEXT:
                        fold(chunk, part, d).start()

    def add_first(chunk):
        for part in range(2):
            for d in NEXT:
                first_sum(chunk, part, d).wait_recv()
            summed[chunk, part] = (
                ladder[chunk, part, 0] + level1[chunk, part, 0]
            ) + level1[chunk, part, 1]
            for d in SHIFTS:
                second_sum(chunk, part, d).start()

    def add_second(chunk):
        for part in range(2):
            for d in SHIFTS:
                second_sum(chunk, part, d).wait_recv()
            at = pl.ds(
                pl.multiple_of((chunk * 2 + (other if part else core)) * ROWS, ROWS), ROWS
            )
            out_ref[at, :] = (summed[chunk, part, 0:ROWS, :] + level2[chunk, part, 0]) + (
                level2[chunk, part, 1] + level2[chunk, part, 2]
            )

    v_copy = pltpu.make_async_copy(v_ref, v_raw, v_sem)
    v_copy.start()

    barrier = pltpu.get_barrier_semaphore()
    greeted = [(da, db, 0) for da, db in SPREAD[:-1]] + [(0, 0, 1)]
    for da, db, flip in greeted:
        pl.semaphore_signal(barrier, inc=1, device_id=device(da, db, flip), device_id_type=MESH)
    pl.semaphore_wait(barrier, len(greeted))

    for chunk in range(CHUNKS):
        swap(chunk).start()
    for chunk in range(CHUNKS):
        start_spread(chunk, 0)
        swap(chunk).wait()
        start_spread(chunk, 1)

    v_copy.wait()
    tile = 256

    @pl.loop(0, v_raw.shape[1] // tile)
    def _(n):
        cd = pl.ds(pl.multiple_of(n * tile, tile), tile)
        for m in range(0, v_raw.shape[0], tile):
            value = v_raw[m:m + tile, cd]
            high = value.astype(jnp.bfloat16)
            low = (value - high.astype(jnp.float32)).astype(jnp.bfloat16)
            v_hi[cd, m:m + tile] = high.T
            v_lo[cd, m:m + tile] = low.T

    for chunk in range(CHUNKS):
        start_collect(chunk)
    for chunk in range(CHUNKS):
        forward_collect(chunk)
    ahead = None
    for da in GROUPS:
        for chunk in range(CHUNKS):
            exchange(chunk, da)
            if ahead:
                multiply(*ahead)
            ahead = (chunk, da)
    multiply(*ahead)
    for chunk in range(CHUNKS):
        add_first(chunk)
    for chunk in range(CHUNKS):
        add_second(chunk)

    for chunk in range(CHUNKS):
        for da in range(SIDE):
            for db in range(SIDE):
                for flip in range(2):
                    if (da, db) != (0, 0):
                        spread(chunk, da, db, flip).wait_send()
                if db:
                    collect_b(chunk, da, db).wait_send()
                share(chunk, da, db).wait_send()
        for d in SHIFTS:
            collect_a(chunk, d).wait_send()
            for part in range(2):
                second_sum(chunk, part, d).wait_send()
                if d in NEXT:
                    first_sum(chunk, part, d).wait_send()
                    fold(chunk, part, d).wait_send()


def per_device(t2_stored, v_slab, block_source, r_in):
    ab, cd = v_slab.shape
    blocks = block_source.shape[0]
    stored = t2_stored.shape[1] // BLK
    owned = cd // BLK
    tiles = t2_stored.reshape(-1, ROWS, stored, BLK).transpose(0, 2, 1, 3)
    tiles = tiles.reshape(SLABS, CHUNKS, 2, stored, ROWS, BLK)
    group = SIDE * ROWS
    f32, bf16 = jnp.float32, jnp.bfloat16
    dma = pltpu.SemaphoreType.DMA
    ladder = pl.pallas_call(
        kernel,
        out_shape=jax.ShapeDtypeStruct(r_in.shape, f32),
        in_specs=[
            pl.BlockSpec(memory_space=pltpu.SMEM),
            pl.BlockSpec(memory_space=pl.ANY),
            pl.BlockSpec(memory_space=pl.ANY),
        ],
        out_specs=pl.BlockSpec(memory_space=pltpu.VMEM),
        scratch_shapes=[
            pltpu.VMEM((ab, cd), f32),
            pltpu.VMEM((cd, ab), bf16),
            pltpu.VMEM((cd, ab), bf16),
            pltpu.VMEM((CHUNKS, SLABS, stored, ROWS, BLK), f32),
            pltpu.VMEM((blocks, ROWS, BLK), f32),
            pltpu.VMEM((blocks, ROWS, BLK), f32),
            pltpu.VMEM((CHUNKS, SIDE - 1, SIDE, ROWS, cd), f32),
            pltpu.VMEM((CHUNKS, SIDE, SIDE, ROWS, cd), f32),
            pltpu.VMEM((CHUNKS, 2, SIDE, SIDE, ROWS, cd), f32),
            pltpu.VMEM((4 * group, cd), bf16),
            pltpu.VMEM((CHUNKS, 2, SIDE, group, ab), f32),
            pltpu.VMEM((CHUNKS, 2, 2, group // 2, ab), f32),
            pltpu.VMEM((CHUNKS, 2, 2, group, ab), f32),
            pltpu.VMEM((CHUNKS, 2, group, ab), f32),
            pltpu.VMEM((CHUNKS, 2, SIDE - 1, ROWS, ab), f32),
            dma,
            dma((4 * CHUNKS,)),
            dma((CHUNKS, 2 * SIDE)),
            dma((CHUNKS, 2 * SLABS)),
            dma((CHUNKS, 2 * SLABS)),
            dma((CHUNKS, SIDE - 1)),
            dma((CHUNKS, SIDE - 1)),
            dma((CHUNKS, SIDE, SIDE - 1)),
            dma((CHUNKS, SIDE, SIDE - 1)),
            dma((CHUNKS, SIDE, SIDE)),
            dma((CHUNKS, SIDE, SIDE)),
            dma((CHUNKS, 2, 2)),
            dma((CHUNKS, 2, 2)),
            dma((CHUNKS, 2, SIDE - 1)),
            dma((CHUNKS, 2, SIDE - 1)),
            dma((CHUNKS, 2, 2)),
            dma((CHUNKS, 2, 2)),
        ],
        compiler_params=pltpu.CompilerParams(
            collective_id=1, has_side_effects=True, vmem_limit_bytes=60 * 1024 * 1024
        ),
        name="ladder",
    )(block_source, tiles, v_slab)
    return r_in + ladder


def solution(mesh):
    in_specs = (P("row", ("slab", "rep")), P("rep", "slab"), P(), P(("row", "slab"), "rep"))
    out_specs = P(("row", "slab"), "rep")
    return jax.shard_map(
        per_device, mesh=mesh, in_specs=in_specs, out_specs=out_specs, check_vma=False
    )
```

```python
import jax
import jax.numpy as jnp
from jax import lax
from jax.experimental import pallas as pl
from jax.experimental.pallas import tpu as pltpu
from jax.sharding import PartitionSpec as P

BLK = 128
SIDE = 4
SLABS = 16
CHUNKS = 2
ROWS = 8
MESH = pl.DeviceIdType.MESH


SHIFTS = (2, 1, 3)
ARRIVALS = (2, 1, 3)
NEXT = (1, 3)
SPREAD = sorted(
    [(da, db) for da in range(SIDE) for db in range(SIDE)],
    key=lambda d: -sum(min(n, SIDE - n) for n in d),
)
GROUPS = (2, 1, 3, 0)


def kernel(
    source_ref, t2_ref, v_ref, out_ref,
    v_raw, v_hi, v_lo, swapped, part_a, part_b, send_buf, relay2, whole, split,
    ladder, folded, level1, summed, level2,
    v_sem, swap_sem, own_sem, send1, recv1, send3, recv3, send4, recv4,
    send5, recv5, send6, recv6, send7, recv7, send8, recv8,
):
    row = lax.axis_index("row")
    slab = lax.axis_index("slab")
    core = lax.axis_index("rep")
    x, y = slab // SIDE, slab % SIDE
    a = x + core * (y - x)
    b = y + core * (x - y)
    a_step = SIDE - core * (SIDE - 1)
    b_step = 1 + core * (SIDE - 1)
    to_a = [(a + d) & (SIDE - 1) for d in range(SIDE)]
    to_b = [(b + d) & (SIDE - 1) for d in range(SIDE)]
    a_term = [n * a_step for n in to_a]
    b_term = [n * b_step for n in to_b]
    b_all = [n * b_step for n in range(SIDE)]
    other = 1 - core
    stored = t2_ref.shape[3]
    owned = v_ref.shape[1] // BLK
    group = SIDE * ROWS
    half = group // 2
    parts = (part_a, part_b)

    def device(da, db, flip=0):
        return (row, a_term[da % SIDE] + b_term[db % SIDE], other if flip else core)

    def remote(src, dst, send_sem, recv_sem, da, db, flip=0):
        return pltpu.make_async_remote_copy(
            src_ref=src,
            dst_ref=dst,
            send_sem=send_sem,
            recv_sem=recv_sem,
            device_id=device(da, db, flip),
            device_id_type=MESH,
        )

    def swap(chunk):
        return remote(
            t2_ref.at[:, chunk, other],
            swapped.at[chunk],
            swap_sem.at[2 * chunk],
            swap_sem.at[2 * chunk + 1],
            0,
            0,
            1,
        )

    def spread(chunk, da, db, flip):
        to_slab = a_term[da] + b_term[db]
        if flip:
            src = swapped.at[chunk, to_slab]
        else:
            src = t2_ref.at[to_slab, chunk, core]
        holder = slab * 2 + (other if flip else core)
        dst = parts[chunk].at[pl.ds(holder * stored, stored)]
        if (da, db) == (0, 0):
            return pltpu.make_async_copy(src, dst, swap_sem.at[4 + 2 * chunk + flip])
        n = (da * SIDE + db) * 2 + flip
        return remote(src, dst, send1.at[chunk, n], recv1.at[chunk, n], da, db)

    def spread_arrival(chunk, da, db, flip):
        holder = (a_term[-da % SIDE] + b_term[-db % SIDE]) * 2 + (other if flip else core)
        here = parts[chunk].at[pl.ds(holder * stored, stored)]
        n = (da * SIDE + db) * 2 + flip
        return remote(here, here, send1.at[chunk, n], recv1.at[chunk, n], da, db)

    def collect_a(chunk, da):
        return remote(
            send_buf.at[chunk, da - 1],
            relay2.at[chunk, :, da],
            send3.at[chunk, da - 1],
            recv3.at[chunk, da - 1],
            da,
            0,
        )

    def collect_b(chunk, da, db):
        src = relay2.at[chunk, to_b[db], da]
        dst = whole.at[chunk, 0, da, db]
        if db == 0:
            return pltpu.make_async_copy(src, dst, own_sem.at[chunk, SIDE + da])
        n = db - 1
        return remote(src, dst, send4.at[chunk, da, n], recv4.at[chunk, da, n], 0, db)

    def share(chunk, da, db):
        src = relay2.at[chunk, b, da] if db == 0 else whole.at[chunk, 0, da, db]
        dst = whole.at[chunk, 1, da, db]
        return remote(src, dst, send5.at[chunk, da, db], recv5.at[chunk, da, db], 0, 0, 1)

    def fold(chunk, part, d):
        n = d // 2
        return remote(
            ladder.at[chunk, part, 2, pl.ds(n * half, half)],
            folded.at[chunk, part, n],
            send8.at[chunk, part, n],
            recv8.at[chunk, part, n],
            *((-d, 0), (0, -d))[part],
        )

    def first_sum(chunk, part, d):
        n = d // 2
        return remote(
            ladder.at[chunk, part, d],
            level1.at[chunk, part, n],
            send6.at[chunk, part, n],
            recv6.at[chunk, part, n],
            *((-d, 0), (0, -d))[part],
        )

    def second_sum(chunk, part, d):
        return remote(
            summed.at[chunk, part, pl.ds(d * ROWS, ROWS)],
            level2.at[chunk, part, d - 1],
            send7.at[chunk, part, d - 1],
            recv7.at[chunk, part, d - 1],
            *((0, -d), (-d, 0))[part],
        )

    def start_spread(chunk, flip):
        for da, db in SPREAD:
            spread(chunk, da, db, flip).start()

    def forward_blocks(chunk, da):
        for db in SHIFTS + (0,):
            collect_b(chunk, da, db).start()
        share(chunk, da, 0).start()

    def start_collect(chunk):
        for da, db in SPREAD:
            for flip in range(2):
                if (da, db) == (0, 0):
                    spread(chunk, 0, 0, flip).wait()
                else:
                    spread_arrival(chunk, da, db, flip).wait_recv()
        for da in SHIFTS + (0,):
            for its_b in range(SIDE):
                first = (a_term[da] + b_all[its_b]) * owned
                for k in range(owned):
                    piece = parts[chunk][source_ref[first + k]]
                    cols = slice(k * BLK, (k + 1) * BLK)
                    if da == 0:
                        relay2[chunk, its_b, 0, :, cols] = piece
                    else:
                        send_buf[chunk, da - 1, its_b, :, cols] = piece
            if da:
                collect_a(chunk, da).start()
        forward_blocks(chunk, 0)

    def forward_collect(chunk):
        for da in ARRIVALS:
            collect_a(chunk, da).wait_recv()
            forward_blocks(chunk, da)

    def exchange(chunk, da):
        for db in ARRIVALS:
            collect_b(chunk, da, db).wait_recv()
            share(chunk, da, db).start()

    def multiply(chunk, da):
        collect_b(chunk, da, 0).wait()
        for db in range(SIDE):
            share(chunk, da, db).wait_recv()
        value = whole[chunk, :, da].reshape(2 * group, v_hi.shape[0])
        high = value.astype(jnp.bfloat16)
        split[0:2 * group, :] = high
        split[2 * group:, :] = (value - high.astype(jnp.float32)).astype(jnp.bfloat16)
        dims = (((1,), (0,)), ((), ()))
        both = lax.dot_general(
            split[...], v_hi[...], dims, preferred_element_type=jnp.float32
        )
        low = lax.dot_general(
            split[0:2 * group, :], v_lo[...], dims, preferred_element_type=jnp.float32
        )
        total = both[0:2 * group] + (both[2 * group:] + low)
        for part in range(2):
            at = part * group
            if da in NEXT:
                fold(chunk, part, da).wait_recv()
                n = da // 2
                near = slice(n * half, (n + 1) * half)
                far = slice((1 - n) * half, (2 - n) * half)
                ladder[chunk, part, da, near] = (
                    total[at + n * half:at + (n + 1) * half] + folded[chunk, part, n]
                )
                ladder[chunk, part, da, far] = total[at + (1 - n) * half:at + (2 - n) * half]
                first_sum(chunk, part, da).start()
            else:
                ladder[chunk, part, da] = total[at:at + group]
                if da:
                    for d in NEXT:
                        fold(chunk, part, d).start()

    def add_first(chunk):
        for part in range(2):
            for d in NEXT:
                first_sum(chunk, part, d).wait_recv()
            summed[chunk, part] = (
                ladder[chunk, part, 0] + level1[chunk, part, 0]
            ) + level1[chunk, part, 1]
            for d in SHIFTS:
                second_sum(chunk, part, d).start()

    def add_second(chunk):
        for part in range(2):
            for d in SHIFTS:
                second_sum(chunk, part, d).wait_recv()
            at = pl.ds(
                pl.multiple_of((chunk * 2 + (other if part else core)) * ROWS, ROWS), ROWS
            )
            out_ref[at, :] = (summed[chunk, part, 0:ROWS, :] + level2[chunk, part, 0]) + (
                level2[chunk, part, 1] + level2[chunk, part, 2]
            )

    v_copy = pltpu.make_async_copy(v_ref, v_raw, v_sem)
    v_copy.start()

    barrier = pltpu.get_barrier_semaphore()
    greeted = [(da, db, 0) for da, db in SPREAD[:-1]] + [(0, 0, 1)]
    for da, db, flip in greeted:
        pl.semaphore_signal(barrier, inc=1, device_id=device(da, db, flip), device_id_type=MESH)
    pl.semaphore_wait(barrier, len(greeted))

    for chunk in range(CHUNKS):
        swap(chunk).start()
    for chunk in range(CHUNKS):
        start_spread(chunk, 0)
        swap(chunk).wait()
        start_spread(chunk, 1)

    v_copy.wait()
    tile = 256

    @pl.loop(0, v_raw.shape[1] // tile)
    def _(n):
        cd = pl.ds(pl.multiple_of(n * tile, tile), tile)
        for m in range(0, v_raw.shape[0], tile):
            value = v_raw[m:m + tile, cd]
            high = value.astype(jnp.bfloat16)
            low = (value - high.astype(jnp.float32)).astype(jnp.bfloat16)
            v_hi[cd, m:m + tile] = high.T
            v_lo[cd, m:m + tile] = low.T

    for chunk in range(CHUNKS):
        start_collect(chunk)
    for chunk in range(CHUNKS):
        forward_collect(chunk)
    for da in GROUPS:
        for chunk in range(CHUNKS):
            exchange(chunk, da)
        for chunk in range(CHUNKS):
            multiply(chunk, da)
    for chunk in range(CHUNKS):
        add_first(chunk)
    for chunk in range(CHUNKS):
        add_second(chunk)

    for chunk in range(CHUNKS):
        for da in range(SIDE):
            for db in range(SIDE):
                for flip in range(2):
                    if (da, db) != (0, 0):
                        spread(chunk, da, db, flip).wait_send()
                if db:
                    collect_b(chunk, da, db).wait_send()
                share(chunk, da, db).wait_send()
        for d in SHIFTS:
            collect_a(chunk, d).wait_send()
            for part in range(2):
                second_sum(chunk, part, d).wait_send()
                if d in NEXT:
                    first_sum(chunk, part, d).wait_send()
                    fold(chunk, part, d).wait_send()


def per_device(t2_stored, v_slab, block_source, r_in):
    ab, cd = v_slab.shape
    blocks = block_source.shape[0]
    stored = t2_stored.shape[1] // BLK
    owned = cd // BLK
    tiles = t2_stored.reshape(-1, ROWS, stored, BLK).transpose(0, 2, 1, 3)
    tiles = tiles.reshape(SLABS, CHUNKS, 2, stored, ROWS, BLK)
    group = SIDE * ROWS
    f32, bf16 = jnp.float32, jnp.bfloat16
    dma = pltpu.SemaphoreType.DMA
    ladder = pl.pallas_call(
        kernel,
        out_shape=jax.ShapeDtypeStruct(r_in.shape, f32),
        in_specs=[
            pl.BlockSpec(memory_space=pltpu.SMEM),
            pl.BlockSpec(memory_space=pl.ANY),
            pl.BlockSpec(memory_space=pl.ANY),
        ],
        out_specs=pl.BlockSpec(memory_space=pltpu.VMEM),
        scratch_shapes=[
            pltpu.VMEM((ab, cd), f32),
            pltpu.VMEM((cd, ab), bf16),
            pltpu.VMEM((cd, ab), bf16),
            pltpu.VMEM((CHUNKS, SLABS, stored, ROWS, BLK), f32),
            pltpu.VMEM((blocks, ROWS, BLK), f32),
            pltpu.VMEM((blocks, ROWS, BLK), f32),
            pltpu.VMEM((CHUNKS, SIDE - 1, SIDE, ROWS, cd), f32),
            pltpu.VMEM((CHUNKS, SIDE, SIDE, ROWS, cd), f32),
            pltpu.VMEM((CHUNKS, 2, SIDE, SIDE, ROWS, cd), f32),
            pltpu.VMEM((4 * group, cd), bf16),
            pltpu.VMEM((CHUNKS, 2, SIDE, group, ab), f32),
            pltpu.VMEM((CHUNKS, 2, 2, group // 2, ab), f32),
            pltpu.VMEM((CHUNKS, 2, 2, group, ab), f32),
            pltpu.VMEM((CHUNKS, 2, group, ab), f32),
            pltpu.VMEM((CHUNKS, 2, SIDE - 1, ROWS, ab), f32),
            dma,
            dma((4 * CHUNKS,)),
            dma((CHUNKS, 2 * SIDE)),
            dma((CHUNKS, 2 * SLABS)),
            dma((CHUNKS, 2 * SLABS)),
            dma((CHUNKS, SIDE - 1)),
            dma((CHUNKS, SIDE - 1)),
            dma((CHUNKS, SIDE, SIDE - 1)),
            dma((CHUNKS, SIDE, SIDE - 1)),
            dma((CHUNKS, SIDE, SIDE)),
            dma((CHUNKS, SIDE, SIDE)),
            dma((CHUNKS, 2, 2)),
            dma((CHUNKS, 2, 2)),
            dma((CHUNKS, 2, SIDE - 1)),
            dma((CHUNKS, 2, SIDE - 1)),
            dma((CHUNKS, 2, 2)),
            dma((CHUNKS, 2, 2)),
        ],
        compiler_params=pltpu.CompilerParams(
            collective_id=1, has_side_effects=True, vmem_limit_bytes=60 * 1024 * 1024
        ),
        name="ladder",
    )(block_source, tiles, v_slab)
    return r_in + ladder


def solution(mesh):
    in_specs = (P("row", ("slab", "rep")), P("rep", "slab"), P(), P(("row", "slab"), "rep"))
    out_specs = P(("row", "slab"), "rep")
    return jax.shard_map(
        per_device, mesh=mesh, in_specs=in_specs, out_specs=out_specs, check_vma=False
    )
```
